32 devices in a mesh: groups: 2 (over y), blk: 16 (over z, x, core).
Axes of the slice: x: 2, y: 2, z: 4, core: 2. Of those that a mesh axis runs over, the one named last changes fastest.
Arguments:
- psi: bfloat16 [64, 512, 512], P(('groups', 'blk')), parts along dimension 0, may hold values from -6 to 6
- sector_size: int32 [64], P('groups'), parts along dimension 0, may hold values from 1 to 512, 8192 in all
- source: int32 [32, 32], P('groups'), parts along dimension 0, may hold values from 0 to 31, each once within a row
- left_env: bfloat16 [16, 64, 512], P(None, 'groups', 'blk'), parts along dimension 1, may hold values from -3 to 3
- right_env: bfloat16 [32, 512, 512], P('groups'), parts along dimension 0, may hold values from -0.25 to 0.25
Outputs:
- hpsi: bfloat16 [64, 512, 512], P(('groups', 'blk')), parts along dimension 0
The draws below stay inside these ranges and needn't reach their ends.
There are 2 independent parts, one for each index of `groups`. The reference program is written for one: setup_inputs(seed, part) draws one part's arguments, and reference() takes and returns one part's arrays. A program takes and returns all parts, laid end to end along the dimension named above; each array names one. Nothing has to cross between parts.
Inputs may be any that keep to these rules, and one draw needn't show every extreme that they name: Each row of source is a permutation of the 32 sector blocks. `sector_size`: the sizes sum to 8192.
All inputs are finite; a program needn't handle non-finite values.
Results may differ from the reference program's by a relative error of at most 0.0049.
Values may be sent and summed in bfloat16 or wider, within the bound.
A program may use at most 128 MiB of HBM per device.

```python
import math
import jax
import jax.numpy as jnp
import numpy as np
from jax import lax

B = 512
K = 512
NW = 16
S = 32


def block_scale(stream_key, extent, pieces, low, largest):
    loudness, own = 1.0, jax.random.fold_in(stream_key, 6)
    for dim, blocks in pieces:
        heights = jnp.exp(jax.random.uniform(jax.random.fold_in(own, dim), (blocks,), jnp.float32, low / len(pieces), largest / len(pieces)))
        loudness = loudness * jnp.repeat(heights, extent[dim] // blocks).reshape([-1 if axis == dim else 1 for axis in range(len(extent))])
    return loudness


def profile(number_of, total, bound, lean):
    loads = [(1 << 20) // math.isqrt(standing ** lean) + 1 for standing in range(2, number_of + 1)]
    spare, counts = total - bound - (number_of - 1), [1] * (number_of - 1)
    while spare > 0:
        candidates = [i for i in range(number_of - 1) if counts[i] < bound]
        mass, budget = sum([loads[i] for i in candidates]), spare
        for i in candidates:
            more = min(bound - counts[i], max(1, budget * loads[i] // mass), spare)
            counts[i] = counts[i] + more
            spare = spare - more
    return np.array([bound] + counts)


def uneven(key, number_of, total, bound, slope):
    if number_of == 2:
        one = jax.random.randint(key, (), max(1, total - bound), min(bound, total - 1) + 1)
        return jnp.stack([one, total - one])
    tallies = jnp.asarray(profile(number_of, total, bound, slope), jnp.int32)
    pairs = (number_of - 1) // 2
    donor, taker = tallies[1:1 + 2 * pairs:2], tallies[2:2 + 2 * pairs:2]
    margin = jnp.minimum(donor - 1, bound - taker)
    shifted = jax.random.randint(jax.random.fold_in(key, 1), (pairs,), 0, 1 << 20) % (margin + 1)
    tallies = tallies.at[1:1 + 2 * pairs:2].set(donor - shifted).at[2:2 + 2 * pairs:2].set(taker + shifted)
    return tallies[jax.random.permutation(jax.random.fold_in(key, 2), number_of)]


def normal_values(rng, dims, deviation, bound, pieces=(), kind=jnp.bfloat16):
    entries = deviation * jax.random.normal(rng, dims, jnp.float32)
    if pieces:
        entries = entries * block_scale(rng, dims, pieces, -0.22, 0.18)
    return jnp.clip(entries, -bound, bound).astype(kind)


def setup_inputs(seed: int = 0, part: int = 0) -> dict:
    splits = jax.random.split(jax.random.key(seed), 6)
    own_keys = jax.random.split(jax.random.fold_in(splits[5], part), 6)
    return {
        "psi": normal_values(own_keys[0], (S, B, K), 1.0, 6.0, ((0, 16),)),
        "sector_size": uneven(own_keys[1], S, S * B // 2, B, 0).astype(jnp.int32),
        "source": jax.vmap(lambda own: jax.random.permutation(own, S))(jax.random.split(own_keys[2], NW)).reshape((NW, S)).astype(jnp.int32),
        "left_env": normal_values(own_keys[3], (NW, S, B), 0.5, 3.0, ((2, 16),)),
        "right_env": normal_values(own_keys[4], (NW, K, K), K ** -0.5, 0.25),
    }


def reference(psi, sector_size, source, left_env, right_env):
    rows = jnp.arange(B, dtype=jnp.int32)
    keep = (rows[None, :] < sector_size[:, None])
    masked = jnp.where(keep[:, :, None], psi, jnp.zeros_like(psi))
    flat = masked.reshape(S * B, K)

    def one_term(total, index):
        projected = jnp.dot(flat, right_env[index], preferred_element_type=jnp.float32).astype(jnp.bfloat16)
        picked = projected.reshape(S, B, K)[source[index]]
        coeff = left_env[index].astype(jnp.float32)
        return total + coeff[:, :, None] * picked.astype(jnp.float32), None

    total, _ = lax.scan(one_term, jnp.zeros((S, B, K), jnp.float32), jnp.arange(NW, dtype=jnp.int32))
    return jnp.where(keep[:, :, None], total, jnp.zeros_like(total)).astype(jnp.bfloat16)
```

```python
import functools

import jax
import jax.numpy as jnp
from jax import lax
from jax.experimental import pallas as pl
from jax.experimental.pallas import tpu as pltpu
from jax.sharding import PartitionSpec as P

MESH = pl.DeviceIdType.MESH
CHUNK = 16
LANES = 128


def kernel(n, sizes, source, left, psi, right, out, recv, moved, res, coef, lhs, weights, fs, fr, bs, br, ls, lb, ws):
    me = lax.axis_index("blk")
    own, rows_all, width = psi.shape
    terms, sectors = source.shape
    per_rows = rows_all // n
    chunks = per_rows // CHUNK

    def peer_of(step):
        shift = n // 2 + (1 - 2 * (step % 2)) * ((step + 1) // 2)
        return lax.rem(me + shift, n)

    def slot(device):
        return pl.ds(device * own, own)

    def rows_of(device, c):
        return pl.ds(pl.multiple_of(device * per_rows + c * CHUNK, CHUNK), CHUNK)

    def forward(c, peer, landing):
        return pltpu.make_async_remote_copy(
            src_ref=psi.at[:, rows_of(peer, c), :],
            dst_ref=recv.at[c, slot(landing)],
            send_sem=fs.at[c, peer],
            recv_sem=fr.at[c, landing],
            device_id={"blk": peer},
            device_id_type=MESH,
        )

    def backward(c, peer, landing):
        return pltpu.make_async_remote_copy(
            src_ref=res.at[c, slot(peer)],
            dst_ref=out.at[:, rows_of(landing, c), :],
            send_sem=bs.at[c, peer],
            recv_sem=br.at[c, landing],
            device_id={"blk": peer},
            device_id_type=MESH,
        )

    def own_in(c):
        return pltpu.make_async_copy(psi.at[:, rows_of(me, c), :], recv.at[c, slot(me)], ls.at[c])

    def own_out(c):
        return pltpu.make_async_copy(res.at[c, slot(me)], out.at[:, rows_of(me, c), :], lb.at[c])

    def each_peer(action):
        def step(k, carry):
            action(peer_of(k))
            return carry

        lax.fori_loop(0, n - 1, step, 0)

    load = pltpu.make_async_copy(right, weights, ws)
    barrier = pltpu.get_barrier_semaphore()
    each_peer(lambda peer: pl.semaphore_signal(barrier, inc=1, device_id={"blk": peer}, device_id_type=MESH))
    pl.semaphore_wait(barrier, n - 1)

    for c in range(chunks):
        each_peer(lambda peer: forward(c, peer, me).start())
    for c in range(chunks):
        own_in(c).start()
    load.start()

    row = lax.broadcasted_iota(jnp.int32, (per_rows, LANES), 0) + me * per_rows
    unit = (
        lax.broadcasted_iota(jnp.int32, (per_rows, per_rows), 0)
        == lax.broadcasted_iota(jnp.int32, (per_rows, per_rows), 1)
    ).astype(jnp.float32).astype(jnp.bfloat16)

    def spread(w, carry):
        turned = lax.dot_general(
            unit, left[w], (((1,), (1,)), ((), ())), preferred_element_type=jnp.float32
        )
        for s in range(sectors):
            column = jnp.broadcast_to(turned[:, s : s + 1], (per_rows, LANES))
            coef[w, s] = jnp.where(row < sizes[s], column, 0.0).astype(jnp.bfloat16)
        return carry

    lax.fori_loop(0, terms, spread, 0)

    row16 = lax.broadcasted_iota(jnp.int32, (CHUNK, width), 0) + me * per_rows
    for c in range(chunks):
        own_in(c).wait()
        each_peer(lambda peer: forward(c, peer, peer).wait_recv())

        def mask(s, carry):
            value = recv[c, s].astype(jnp.float32)
            moved[s] = jnp.where(row16 + c * CHUNK < sizes[s], value, 0.0).astype(jnp.bfloat16)
            return carry

        lax.fori_loop(0, sectors, mask, 0)

        def build(w, carry):
            columns = pl.ds(pl.multiple_of(w * width, width), width)
            for s in range(sectors):
                factor = coef[w, s, c * CHUNK : (c + 1) * CHUNK, :]
                factor = jnp.concatenate([factor] * (width // LANES), axis=1)
                lhs[s * CHUNK : (s + 1) * CHUNK, columns] = moved[source[w, s]] * factor
            return carry

        lax.fori_loop(0, terms, build, 0)
        if c == 0:
            load.wait()
        tall = weights.reshape(terms * width, width)
        half = width // 2
        for part in range(2):
            cols = slice(part * half, (part + 1) * half)
            total = jnp.dot(lhs[...], tall[:, cols], preferred_element_type=jnp.float32)
            res[c, :, :, cols] = total.astype(jnp.bfloat16).reshape(sectors, CHUNK, half)
        each_peer(lambda peer: backward(c, peer, me).start())
        own_out(c).start()

    for c in range(chunks):
        each_peer(lambda peer: forward(c, peer, me).wait_send())
        each_peer(lambda peer: backward(c, peer, me).wait_send())
        own_out(c).wait()
        each_peer(lambda peer: backward(c, peer, peer).wait_recv())


def fused(psi, sector_size, source, left_env, right_env):
    n = lax.axis_size("blk")
    own, rows_all, width = psi.shape
    terms, sectors = source.shape
    per_rows = rows_all // n
    chunks = per_rows // CHUNK
    rows = sectors * CHUNK
    smem = pl.BlockSpec(memory_space=pltpu.SMEM)
    vmem = pl.BlockSpec(memory_space=pltpu.VMEM)
    anywhere = pl.BlockSpec(memory_space=pl.ANY)
    return pl.pallas_call(
        functools.partial(kernel, n),
        out_shape=jax.ShapeDtypeStruct(psi.shape, jnp.bfloat16),
        in_specs=[smem, smem, vmem, anywhere, anywhere],
        out_specs=anywhere,
        scratch_shapes=[
            pltpu.VMEM((chunks, sectors, CHUNK, width), jnp.bfloat16),
            pltpu.VMEM((sectors, CHUNK, width), jnp.bfloat16),
            pltpu.VMEM((chunks, sectors, CHUNK, width), jnp.bfloat16),
            pltpu.VMEM((terms, sectors, per_rows, LANES), jnp.bfloat16),
            pltpu.VMEM((rows, terms * width), jnp.bfloat16),
            pltpu.VMEM((terms, width, width), jnp.bfloat16),
            pltpu.SemaphoreType.DMA((chunks, n)),
            pltpu.SemaphoreType.DMA((chunks, n)),
            pltpu.SemaphoreType.DMA((chunks, n)),
            pltpu.SemaphoreType.DMA((chunks, n)),
            pltpu.SemaphoreType.DMA((chunks,)),
            pltpu.SemaphoreType.DMA((chunks,)),
            pltpu.SemaphoreType.DMA,
        ],
        compiler_params=pltpu.CompilerParams(
            collective_id=0, has_side_effects=True, vmem_limit_bytes=48 << 20
        ),
        cost_estimate=pl.CostEstimate(
            flops=2 * terms * sectors * per_rows * width * width,
            bytes_accessed=right_env.size * 2 + psi.size * 8,
            transcendentals=0,
        ),
    )(sector_size, source, left_env, psi, right_env)


def plain(psi, sector_size, source, left_env, right_env):
    nblk = lax.axis_size("blk")
    me_idx = lax.axis_index("blk")
    sec_local, rows_all, width = psi.shape
    sectors = sector_size.shape[0]
    per_rows = rows_all // nblk
    own_sizes = lax.dynamic_slice_in_dim(sector_size, me_idx * sec_local, sec_local)
    rows = jnp.arange(rows_all, dtype=jnp.int32)
    keep = rows[None, :] < own_sizes[:, None]
    masked = jnp.where(keep[:, :, None], psi, jnp.zeros_like(psi))
    shaped = masked.reshape(sec_local, nblk, per_rows, width)
    moved = lax.all_to_all(shaped, "blk", split_axis=1, concat_axis=0, tiled=True)
    moved = moved.reshape(sectors, per_rows, width)
    gathered = moved[source]
    picked = jnp.einsum(
        "wsrk,wkj->wsrj", gathered, right_env, preferred_element_type=jnp.float32
    ).astype(jnp.bfloat16)
    coeff = left_env.astype(jnp.float32)
    total = jnp.einsum("wsr,wsrj->srj", coeff, picked.astype(jnp.float32))
    global_rows = me_idx * per_rows + jnp.arange(per_rows, dtype=jnp.int32)
    live = global_rows[None, :] < sector_size[:, None]
    result = jnp.where(live[:, :, None], total, jnp.zeros_like(total)).astype(jnp.bfloat16)
    result = result.reshape(sectors, 1, per_rows, width)
    back = lax.all_to_all(result, "blk", split_axis=0, concat_axis=1, tiled=True)
    return back.reshape(sec_local, rows_all, width)


def local(psi, sector_size, source, left_env, right_env):
    per_rows = psi.shape[1] // lax.axis_size("blk")
    run = fused if per_rows % CHUNK == 0 else plain
    return run(psi, sector_size, source, left_env, right_env)


def solution(mesh):
    return jax.shard_map(
        local,
        mesh=mesh,
        in_specs=(
            P(("groups", "blk"), None, None),
            P("groups"),
            P("groups", None),
            P(None, "groups", "blk"),
            P("groups", None, None),
        ),
        out_specs=P(("groups", "blk"), None, None),
        check_vma=False,
    )
```

```python
import functools

import jax
import jax.numpy as jnp
from jax import lax
from jax.experimental import pallas as pl
from jax.experimental.pallas import tpu as pltpu
from jax.sharding import PartitionSpec as P

MESH = pl.DeviceIdType.MESH
CHUNK = 16
LANES = 128


def kernel(
    n, sizes_in, source_in, left_in, psi, right, out,
    sizes, source, left, recv, moved, res, coef, lhs, weights, fs, fr, bs, br, ls, lb, ws, os,
):
    me = lax.axis_index("blk")
    own, rows_all, width = psi.shape
    terms, sectors = source.shape
    per_rows = rows_all // n
    chunks = per_rows // CHUNK

    def peer_of(step):
        return lax.rem(me + 1 + step, n)

    def slot(device):
        return pl.ds(device * own, own)

    def rows_of(device, c):
        return pl.ds(pl.multiple_of(device * per_rows + c * CHUNK, CHUNK), CHUNK)

    def forward(c, peer, landing):
        return pltpu.make_async_remote_copy(
            src_ref=psi.at[:, rows_of(peer, c), :],
            dst_ref=recv.at[c, slot(landing)],
            send_sem=fs.at[c, peer],
            recv_sem=fr.at[c, landing],
            device_id={"blk": peer},
            device_id_type=MESH,
        )

    def backward(c, peer, landing):
        return pltpu.make_async_remote_copy(
            src_ref=res.at[c, slot(peer)],
            dst_ref=out.at[:, rows_of(landing, c), :],
            send_sem=bs.at[c, peer],
            recv_sem=br.at[c, landing],
            device_id={"blk": peer},
            device_id_type=MESH,
        )

    def own_in(c):
        return pltpu.make_async_copy(psi.at[:, rows_of(me, c), :], recv.at[c, slot(me)], ls.at[c])

    def own_out(c):
        return pltpu.make_async_copy(res.at[c, slot(me)], out.at[:, rows_of(me, c), :], lb.at[c])

    def each_peer(action):
        def step(k, carry):
            action(peer_of(k))
            return carry

        lax.fori_loop(0, n - 1, step, 0)

    load = pltpu.make_async_copy(right, weights, ws)
    operands = [
        pltpu.make_async_copy(sizes_in, sizes, os.at[0]),
        pltpu.make_async_copy(source_in, source, os.at[1]),
        pltpu.make_async_copy(left_in, left, os.at[2]),
    ]
    barrier = pltpu.get_barrier_semaphore()
    each_peer(lambda peer: pl.semaphore_signal(barrier, inc=1, device_id={"blk": peer}, device_id_type=MESH))
    for c in range(chunks):
        own_in(c).start()
    for operand in operands:
        operand.start()
    pl.semaphore_wait(barrier, n - 1)

    for c in range(chunks):
        each_peer(lambda peer: forward(c, peer, me).start())
    load.start()
    for operand in operands:
        operand.wait()

    row = lax.broadcasted_iota(jnp.int32, (per_rows, LANES), 0) + me * per_rows
    unit = (
        lax.broadcasted_iota(jnp.int32, (per_rows, per_rows), 0)
        == lax.broadcasted_iota(jnp.int32, (per_rows, per_rows), 1)
    ).astype(jnp.float32).astype(jnp.bfloat16)

    def spread(w, carry):
        turned = lax.dot_general(
            unit, left[w], (((1,), (1,)), ((), ())), preferred_element_type=jnp.float32
        )
        for s in range(sectors):
            column = jnp.broadcast_to(turned[:, s : s + 1], (per_rows, LANES))
            coef[w, s] = jnp.where(row < sizes[s], column, 0.0).astype(jnp.bfloat16)
        return carry

    lax.fori_loop(0, terms, spread, 0)

    row16 = lax.broadcasted_iota(jnp.int32, (CHUNK, width), 0) + me * per_rows
    for c in range(chunks):
        own_in(c).wait()
        each_peer(lambda peer: forward(c, peer, peer).wait_recv())

        def mask(s, carry):
            value = recv[c, s].astype(jnp.float32)
            moved[s] = jnp.where(row16 + c * CHUNK < sizes[s], value, 0.0).astype(jnp.bfloat16)
            return carry

        lax.fori_loop(0, sectors, mask, 0)

        def build(w, carry):
            columns = pl.ds(pl.multiple_of(w * width, width), width)
            for s in range(sectors):
                factor = coef[w, s, c * CHUNK : (c + 1) * CHUNK, :]
                factor = jnp.concatenate([factor] * (width // LANES), axis=1)
                lhs[s * CHUNK : (s + 1) * CHUNK, columns] = moved[source[w, s]] * factor
            return carry

        lax.fori_loop(0, terms, build, 0)
        if c == 0:
            load.wait()
        tall = weights.reshape(terms * width, width)
        half = width // 2
        for part in range(2):
            cols = slice(part * half, (part + 1) * half)
            total = jnp.dot(lhs[...], tall[:, cols], preferred_element_type=jnp.float32)
            res[c, :, :, cols] = total.astype(jnp.bfloat16).reshape(sectors, CHUNK, half)
        each_peer(lambda peer: backward(c, peer, me).start())
        own_out(c).start()

    for c in range(chunks):
        each_peer(lambda peer: forward(c, peer, me).wait_send())
        each_peer(lambda peer: backward(c, peer, me).wait_send())
        own_out(c).wait()
        each_peer(lambda peer: backward(c, peer, peer).wait_recv())


def fused(psi, sector_size, source, left_env, right_env):
    n = lax.axis_size("blk")
    own, rows_all, width = psi.shape
    terms, sectors = source.shape
    per_rows = rows_all // n
    chunks = per_rows // CHUNK
    rows = sectors * CHUNK
    anywhere = pl.BlockSpec(memory_space=pl.ANY)
    return pl.pallas_call(
        functools.partial(kernel, n),
        out_shape=jax.ShapeDtypeStruct(psi.shape, jnp.bfloat16),
        in_specs=[anywhere] * 5,
        out_specs=anywhere,
        scratch_shapes=[
            pltpu.SMEM(sector_size.shape, jnp.int32),
            pltpu.SMEM(source.shape, jnp.int32),
            pltpu.VMEM(left_env.shape, jnp.bfloat16),
            pltpu.VMEM((chunks, sectors, CHUNK, width), jnp.bfloat16),
            pltpu.VMEM((sectors, CHUNK, width), jnp.bfloat16),
            pltpu.VMEM((chunks, sectors, CHUNK, width), jnp.bfloat16),
            pltpu.VMEM((terms, sectors, per_rows, LANES), jnp.bfloat16),
            pltpu.VMEM((rows, terms * width), jnp.bfloat16),
            pltpu.VMEM((terms, width, width), jnp.bfloat16),
            pltpu.SemaphoreType.DMA((chunks, n)),
            pltpu.SemaphoreType.DMA((chunks, n)),
            pltpu.SemaphoreType.DMA((chunks, n)),
            pltpu.SemaphoreType.DMA((chunks, n)),
            pltpu.SemaphoreType.DMA((chunks,)),
            pltpu.SemaphoreType.DMA((chunks,)),
            pltpu.SemaphoreType.DMA,
            pltpu.SemaphoreType.DMA((3,)),
        ],
        compiler_params=pltpu.CompilerParams(
            collective_id=0, has_side_effects=True, vmem_limit_bytes=62 << 20
        ),
        cost_estimate=pl.CostEstimate(
            flops=2 * terms * sectors * per_rows * width * width,
            bytes_accessed=right_env.size * 2 + psi.size * 8,
            transcendentals=0,
        ),
    )(sector_size, source, left_env, psi, right_env)


def plain(psi, sector_size, source, left_env, right_env):
    nblk = lax.axis_size("blk")
    me_idx = lax.axis_index("blk")
    sec_local, rows_all, width = psi.shape
    sectors = sector_size.shape[0]
    per_rows = rows_all // nblk
    own_sizes = lax.dynamic_slice_in_dim(sector_size, me_idx * sec_local, sec_local)
    rows = jnp.arange(rows_all, dtype=jnp.int32)
    keep = rows[None, :] < own_sizes[:, None]
    masked = jnp.where(keep[:, :, None], psi, jnp.zeros_like(psi))
    shaped = masked.reshape(sec_local, nblk, per_rows, width)
    moved = lax.all_to_all(shaped, "blk", split_axis=1, concat_axis=0, tiled=True)
    moved = moved.reshape(sectors, per_rows, width)
    gathered = moved[source]
    picked = jnp.einsum(
        "wsrk,wkj->wsrj", gathered, right_env, preferred_element_type=jnp.float32
    ).astype(jnp.bfloat16)
    coeff = left_env.astype(jnp.float32)
    total = jnp.einsum("wsr,wsrj->srj", coeff, picked.astype(jnp.float32))
    global_rows = me_idx * per_rows + jnp.arange(per_rows, dtype=jnp.int32)
    live = global_rows[None, :] < sector_size[:, None]
    result = jnp.where(live[:, :, None], total, jnp.zeros_like(total)).astype(jnp.bfloat16)
    result = result.reshape(sectors, 1, per_rows, width)
    back = lax.all_to_all(result, "blk", split_axis=0, concat_axis=1, tiled=True)
    return back.reshape(sec_local, rows_all, width)


def local(psi, sector_size, source, left_env, right_env):
    per_rows = psi.shape[1] // lax.axis_size("blk")
    run = fused if per_rows % CHUNK == 0 else plain
    return run(psi, sector_size, source, left_env, right_env)


def solution(mesh):
    return jax.shard_map(
        local,
        mesh=mesh,
        in_specs=(
            P(("groups", "blk"), None, None),
            P("groups"),
            P("groups", None),
            P(None, "groups", "blk"),
            P("groups", None, None),
        ),
        out_specs=P(("groups", "blk"), None, None),
        check_vma=False,
    )
```

```python
import functools

import jax
import jax.numpy as jnp
from jax import lax
from jax.experimental import pallas as pl
from jax.experimental.pallas import tpu as pltpu
from jax.sharding import PartitionSpec as P

MESH = pl.DeviceIdType.MESH
CHUNK = 16
LANES = 128


def kernel(
    n, sizes_in, source_in, left_in, psi, right, out,
    sizes, source, left, recv, moved, res, coef, lhs, weights, fs, fr, bs, br, ls, lb, ws, os,
):
    me = lax.axis_index("blk")
    own, rows_all, width = psi.shape
    terms, sectors = source.shape
    per_rows = rows_all // n
    chunks = per_rows // CHUNK

    def peer_of(step):
        if n % 4:
            return lax.rem(me + 1 + step, n)
        k = step + 1
        z = lax.rem(me // 4 + k // 4, n // 4)
        x = lax.rem((me % 4) // 2 + (k % 4) // 2, 2)
        core = lax.rem(me % 2 + k % 2, 2)
        return z * 4 + x * 2 + core

    def slot(device):
        return pl.ds(device * own, own)

    def rows_of(device, c):
        return pl.ds(pl.multiple_of(device * per_rows + c * CHUNK, CHUNK), CHUNK)

    def forward(c, peer, landing):
        return pltpu.make_async_remote_copy(
            src_ref=psi.at[:, rows_of(peer, c), :],
            dst_ref=recv.at[c, slot(landing)],
            send_sem=fs.at[c, peer],
            recv_sem=fr.at[c, landing],
            device_id={"blk": peer},
            device_id_type=MESH,
        )

    def backward(c, peer, landing):
        return pltpu.make_async_remote_copy(
            src_ref=res.at[c, slot(peer)],
            dst_ref=out.at[:, rows_of(landing, c), :],
            send_sem=bs.at[c, peer],
            recv_sem=br.at[c, landing],
            device_id={"blk": peer},
            device_id_type=MESH,
        )

    def own_in(c):
        return pltpu.make_async_copy(psi.at[:, rows_of(me, c), :], recv.at[c, slot(me)], ls.at[c])

    def own_out(c):
        return pltpu.make_async_copy(res.at[c, slot(me)], out.at[:, rows_of(me, c), :], lb.at[c])

    def each_peer(action):
        def step(k, carry):
            action(peer_of(k))
            return carry

        lax.fori_loop(0, n - 1, step, 0)

    load = pltpu.make_async_copy(right, weights, ws)
    operands = [
        pltpu.make_async_copy(sizes_in, sizes, os.at[0]),
        pltpu.make_async_copy(source_in, source, os.at[1]),
        pltpu.make_async_copy(left_in, left, os.at[2]),
    ]
    barrier = pltpu.get_barrier_semaphore()
    each_peer(lambda peer: pl.semaphore_signal(barrier, inc=1, device_id={"blk": peer}, device_id_type=MESH))
    for c in range(chunks):
        own_in(c).start()
    for operand in operands:
        operand.start()
    pl.semaphore_wait(barrier, n - 1)

    for c in range(chunks):
        each_peer(lambda peer: forward(c, peer, me).start())
    load.start()
    for operand in operands:
        operand.wait()

    row = lax.broadcasted_iota(jnp.int32, (per_rows, LANES), 0) + me * per_rows
    unit = (
        lax.broadcasted_iota(jnp.int32, (per_rows, per_rows), 0)
        == lax.broadcasted_iota(jnp.int32, (per_rows, per_rows), 1)
    ).astype(jnp.float32).astype(jnp.bfloat16)

    def spread(w, carry):
        turned = lax.dot_general(
            unit, left[w], (((1,), (1,)), ((), ())), preferred_element_type=jnp.float32
        )
        for s in range(sectors):
            column = jnp.broadcast_to(turned[:, s : s + 1], (per_rows, LANES))
            coef[w, s] = jnp.where(row < sizes[s], column, 0.0).astype(jnp.bfloat16)
        return carry

    lax.fori_loop(0, terms, spread, 0)

    row16 = lax.broadcasted_iota(jnp.int32, (CHUNK, width), 0) + me * per_rows
    for c in range(chunks):
        own_in(c).wait()
        each_peer(lambda peer: forward(c, peer, peer).wait_recv())

        def mask(s, carry):
            value = recv[c, s].astype(jnp.float32)
            moved[s] = jnp.where(row16 + c * CHUNK < sizes[s], value, 0.0).astype(jnp.bfloat16)
            return carry

        lax.fori_loop(0, sectors, mask, 0)

        def build(w, carry):
            columns = pl.ds(pl.multiple_of(w * width, width), width)
            for s in range(sectors):
                factor = coef[w, s, c * CHUNK : (c + 1) * CHUNK, :]
                factor = jnp.concatenate([factor] * (width // LANES), axis=1)
                lhs[s * CHUNK : (s + 1) * CHUNK, columns] = moved[source[w, s]] * factor
            return carry

        lax.fori_loop(0, terms, build, 0)
        if c == 0:
            load.wait()
        tall = weights.reshape(terms * width, width)
        half = width // 2
        for part in range(2):
            cols = slice(part * half, (part + 1) * half)
            total = jnp.dot(lhs[...], tall[:, cols], preferred_element_type=jnp.float32)
            res[c, :, :, cols] = total.astype(jnp.bfloat16).reshape(sectors, CHUNK, half)
        each_peer(lambda peer: backward(c, peer, me).start())
        own_out(c).start()

    for c in range(chunks):
        each_peer(lambda peer: forward(c, peer, me).wait_send())
        each_peer(lambda peer: backward(c, peer, me).wait_send())
        own_out(c).wait()
        each_peer(lambda peer: backward(c, peer, peer).wait_recv())


def fused(psi, sector_size, source, left_env, right_env):
    n = lax.axis_size("blk")
    own, rows_all, width = psi.shape
    terms, sectors = source.shape
    per_rows = rows_all // n
    chunks = per_rows // CHUNK
    rows = sectors * CHUNK
    anywhere = pl.BlockSpec(memory_space=pl.ANY)
    return pl.pallas_call(
        functools.partial(kernel, n),
        out_shape=jax.ShapeDtypeStruct(psi.shape, jnp.bfloat16),
        in_specs=[anywhere] * 5,
        out_specs=anywhere,
        scratch_shapes=[
            pltpu.SMEM(sector_size.shape, jnp.int32),
            pltpu.SMEM(source.shape, jnp.int32),
            pltpu.VMEM(left_env.shape, jnp.bfloat16),
            pltpu.VMEM((chunks, sectors, CHUNK, width), jnp.bfloat16),
            pltpu.VMEM((sectors, CHUNK, width), jnp.bfloat16),
            pltpu.VMEM((chunks, sectors, CHUNK, width), jnp.bfloat16),
            pltpu.VMEM((terms, sectors, per_rows, LANES), jnp.bfloat16),
            pltpu.VMEM((rows, terms * width), jnp.bfloat16),
            pltpu.VMEM((terms, width, width), jnp.bfloat16),
            pltpu.SemaphoreType.DMA((chunks, n)),
            pltpu.SemaphoreType.DMA((chunks, n)),
            pltpu.SemaphoreType.DMA((chunks, n)),
            pltpu.SemaphoreType.DMA((chunks, n)),
            pltpu.SemaphoreType.DMA((chunks,)),
            pltpu.SemaphoreType.DMA((chunks,)),
            pltpu.SemaphoreType.DMA,
            pltpu.SemaphoreType.DMA((3,)),
        ],
        compiler_params=pltpu.CompilerParams(
            collective_id=0, has_side_effects=True, vmem_limit_bytes=62 << 20
        ),
        cost_estimate=pl.CostEstimate(
            flops=2 * terms * sectors * per_rows * width * width,
            bytes_accessed=right_env.size * 2 + psi.size * 8,
            transcendentals=0,
        ),
    )(sector_size, source, left_env, psi, right_env)


def plain(psi, sector_size, source, left_env, right_env):
    nblk = lax.axis_size("blk")
    me_idx = lax.axis_index("blk")
    sec_local, rows_all, width = psi.shape
    sectors = sector_size.shape[0]
    per_rows = rows_all // nblk
    own_sizes = lax.dynamic_slice_in_dim(sector_size, me_idx * sec_local, sec_local)
    rows = jnp.arange(rows_all, dtype=jnp.int32)
    keep = rows[None, :] < own_sizes[:, None]
    masked = jnp.where(keep[:, :, None], psi, jnp.zeros_like(psi))
    shaped = masked.reshape(sec_local, nblk, per_rows, width)
    moved = lax.all_to_all(shaped, "blk", split_axis=1, concat_axis=0, tiled=True)
    moved = moved.reshape(sectors, per_rows, width)
    gathered = moved[source]
    picked = jnp.einsum(
        "wsrk,wkj->wsrj", gathered, right_env, preferred_element_type=jnp.float32
    ).astype(jnp.bfloat16)
    coeff = left_env.astype(jnp.float32)
    total = jnp.einsum("wsr,wsrj->srj", coeff, picked.astype(jnp.float32))
    global_rows = me_idx * per_rows + jnp.arange(per_rows, dtype=jnp.int32)
    live = global_rows[None, :] < sector_size[:, None]
    result = jnp.where(live[:, :, None], total, jnp.zeros_like(total)).astype(jnp.bfloat16)
    result = result.reshape(sectors, 1, per_rows, width)
    back = lax.all_to_all(result, "blk", split_axis=0, concat_axis=1, tiled=True)
    return back.reshape(sec_local, rows_all, width)


def local(psi, sector_size, source, left_env, right_env):
    per_rows = psi.shape[1] // lax.axis_size("blk")
    run = fused if per_rows % CHUNK == 0 else plain
    return run(psi, sector_size, source, left_env, right_env)


def solution(mesh):
    return jax.shard_map(
        local,
        mesh=mesh,
        in_specs=(
            P(("groups", "blk"), None, None),
            P("groups"),
            P("groups", None),
            P(None, "groups", "blk"),
            P("groups", None, None),
        ),
        out_specs=P(("groups", "blk"), None, None),
        check_vma=False,
    )
```
